32 devices in a mesh: ta: 4 (over z), gx: 4 (over y, core), yz: 2 (over x).
Axes of the slice: x: 2, y: 2, z: 4, core: 2. Of those that a mesh axis runs over, the one named last changes fastest.
Arguments:
- source: float32 [2, 4, 3, 2, 8, 8, 8, 128], P(None, None, None, None, 'ta', 'gx', 'yz'), may hold values from -6 to 6
- gauge_links: float32 [2, 4, 3, 3, 8, 8, 8, 128], P(None, None, None, None, 'ta', 'gx', 'yz'), may hold values from -1 to 1, as said below
- photon_angles: float32 [4, 8, 8, 8, 128], P(None, 'ta', 'gx', 'yz'), may hold values from -3.140625 to 3.140625
Outputs:
- color_force: float32 [2, 4, 3, 3, 8, 8, 8, 128], P(None, None, None, None, 'ta', 'gx', 'yz')
- photon_force: float32 [4, 8, 8, 8, 128], P(None, 'ta', 'gx', 'yz')
The draws below stay inside these ranges and needn't reach their ends.
Inputs may be any that keep to these rules, and one draw needn't show every extreme that they name: `gauge_links`: every 3x3 link matrix is unitary with determinant one.
All inputs are finite; a program needn't handle non-finite values.
Results may differ from the reference program's by a relative error of at most 0.0001.
Values sent between devices are 32-bit elements; how exact they have to be, the bound alone decides.
A program may use at most 128 MiB of HBM per device.

```python
import jax
import jax.numpy as jnp

NZ = 128
DEGREE = 4
NT = 8
NX = 8
NY = 8


def complex_product(a_re, a_im, b_re, b_im):
    return (a_re * b_re - a_im * b_im, a_re * b_im + a_im * b_re)


def draw_gauge_links(key, part):
    dims_all = (2, 3, 3, 4, NT, NX, NY, NZ)
    raw_draw = jax.random.normal(key, dims_all, jnp.float32)
    row_one = raw_draw[:, 0]
    row_two = raw_draw[:, 1]
    row_one = row_one / jnp.sqrt(jnp.sum(row_one * row_one, axis=(0, 1)))
    inner_re = jnp.sum(row_one[0] * row_two[0] + row_one[1] * row_two[1], axis=0)
    inner_im = jnp.sum(row_one[0] * row_two[1] - row_one[1] * row_two[0], axis=0)
    row_two = row_two - jnp.stack([inner_re * row_one[0] - inner_im * row_one[1], inner_re * row_one[1] + inner_im * row_one[0]])
    row_two = row_two / jnp.sqrt(jnp.sum(row_two * row_two, axis=(0, 1)))
    parts_re = []
    parts_im = []
    for column in range(3):
        next_one = (column + 1) % 3
        next_two = (column + 2) % 3
        left_re, left_im = complex_product(row_one[0][next_one], row_one[1][next_one], row_two[0][next_two], row_two[1][next_two])
        right_re, right_im = complex_product(row_one[0][next_two], row_one[1][next_two], row_two[0][next_one], row_two[1][next_one])
        parts_re.append(left_re - right_re)
        parts_im.append(left_im - right_im)
    row_three = jnp.stack([jnp.stack(parts_re), -jnp.stack(parts_im)])
    matrix = jnp.stack([row_one, row_two, row_three], axis=1)
    return jnp.transpose(matrix, (0, 3, 1, 2, 4, 5, 6, 7))


def steps_of(stream_key, shape, pieces, least, top_value):
    def one(position, shards_of):
        draws = jax.random.uniform(jax.random.fold_in(jax.random.fold_in(stream_key, 6), position), (shards_of,), jnp.float32, least / len(pieces), top_value / len(pieces))
        return jnp.repeat(jnp.exp(draws), shape[position] // shards_of).reshape((-1,) + (1,) * (len(shape) - position - 1))

    factor_of = one(*pieces[0])
    for cut in pieces[1:]:
        factor_of = factor_of * one(*cut)
    return factor_of


def bell_draw(own_key, dims, scale, limit, shards=(), kind=jnp.bfloat16):
    loudness = steps_of(own_key, dims, shards, -0.22, 0.18) if shards else 1.0
    drawn = jax.random.normal(own_key, dims, jnp.float32) * scale * loudness
    return jnp.minimum(jnp.maximum(drawn, -limit), limit).astype(kind)


def setup_inputs(seed: int = 0) -> dict:
    key_list = jax.random.split(jax.random.key(seed), 4)
    return {
        "source": bell_draw(key_list[0], (2, 4, 3, 2, NT, NX, NY, NZ), 1.0, 6.0, ((4, 4), (5, 4), (6, 2)), jnp.float32),
        "gauge_links": draw_gauge_links(jax.random.fold_in(key_list[3], 71), 0),
        "photon_angles": jnp.clip(jax.random.uniform(key_list[2], (4, NT, NX, NY, NZ), jnp.float32, -3.140625, 3.140625), -3.140625, 3.140625),
    }


hopping = 0.15
charge = 2.0 / 3.0


def times_i(values):
    return jnp.stack([-values[1], values[0]])


def matrix_a(lower, course, dagger):
    lower_a = lower[:, 0]
    lower_b = lower[:, 1]
    if course == 0:
        result_a, result_b = -lower_a, -lower_b
    elif course == 1:
        if dagger:
            result_a, result_b = times_i(lower_b), times_i(lower_a)
        else:
            result_a, result_b = -times_i(lower_b), -times_i(lower_a)
    elif course == 2:
        if dagger:
            result_a, result_b = lower_b, -lower_a
        else:
            result_a, result_b = -lower_b, lower_a
    else:
        if dagger:
            result_a, result_b = times_i(lower_a), -times_i(lower_b)
        else:
            result_a, result_b = -times_i(lower_a), times_i(lower_b)
    return jnp.stack([result_a, result_b], axis=1)


def project_minus(spinor, course):
    return spinor[:, :2] - matrix_a(spinor[:, 2:], course, False)


def project_plus(spinor, course):
    return spinor[:, :2] + matrix_a(spinor[:, 2:], course, False)


def rebuild_minus(halfspin, course):
    return jnp.concatenate([halfspin, -matrix_a(halfspin, course, True)], axis=1)


def rebuild_plus(halfspin, course):
    return jnp.concatenate([halfspin, matrix_a(halfspin, course, True)], axis=1)


def gamma_five(spinor):
    signs = jnp.array([1.0, 1.0, -1.0, -1.0], dtype=spinor.dtype).reshape((4, 1, 1, 1, 1, 1, 1))
    return spinor * signs


def color_apply(link_re, link_im, halfspin, dagger):
    if dagger:
        link_re = jnp.swapaxes(link_re, 0, 1)
        link_im = -jnp.swapaxes(link_im, 0, 1)
    copy_sign = jnp.array([1.0, -1.0], dtype=link_re.dtype).reshape((2, 1, 1, 1, 1))
    link_re_wide = link_re[None, :, :, None]
    link_im_wide = link_im[None, :, :, None] * copy_sign
    half_re = halfspin[0][:, None]
    half_im = halfspin[1][:, None]
    real_part = jnp.sum(link_re_wide * half_re - link_im_wide * half_im, axis=2)
    imag_part = jnp.sum(link_re_wide * half_im + link_im_wide * half_re, axis=2)
    return jnp.stack([real_part, imag_part])


def combine_links(gauge_links, photon_angles):
    cosine = jnp.cos(charge * photon_angles)[:, None, None]
    sine = jnp.sin(charge * photon_angles)[:, None, None]
    link_re = cosine * gauge_links[0] - sine * gauge_links[1]
    link_im = cosine * gauge_links[1] + sine * gauge_links[0]
    return link_re, link_im


def outer_product(left, right):
    real_part = jnp.sum(left[0][:, :, None] * right[0][:, None, :] + left[1][:, :, None] * right[1][:, None, :], axis=0)
    imag_part = jnp.sum(left[1][:, :, None] * right[0][:, None, :] - left[0][:, :, None] * right[1][:, None, :], axis=0)
    return real_part, imag_part


def link_force(link_re, link_im, outer_re, outer_im):
    copy_sign = jnp.array([1.0, -1.0], dtype=link_re.dtype).reshape((2, 1, 1, 1, 1))
    left_re = link_re[:, :, None, None]
    left_im = link_im[:, :, None, None] * copy_sign
    prod_re = jnp.sum(left_re * outer_re[None] - left_im * outer_im[None], axis=1)
    prod_im = jnp.sum(left_re * outer_im[None] + left_im * outer_re[None], axis=1)
    merged_re = prod_re[:, :, 0] + prod_re[:, :, 1]
    merged_im = prod_im[:, :, 0] - prod_im[:, :, 1]
    trace_im = merged_im[0, 0] + merged_im[1, 1] + merged_im[2, 2]
    identity = jnp.eye(3, dtype=link_re.dtype).reshape((3, 3, 1, 1, 1, 1))
    anti_re = 0.5 * (merged_re - jnp.swapaxes(merged_re, 0, 1))
    anti_im = 0.5 * (merged_im + jnp.swapaxes(merged_im, 0, 1)) - identity * (trace_im / 3.0)
    return hopping * anti_re, hopping * anti_im, hopping * charge * trace_im


def ahead(field, course):
    axis_no = field.ndim + course - 4
    shifted = jnp.roll(field, -1, axis=axis_no)
    length = field.shape[axis_no]
    if course == 0:
        at_edge = (jnp.arange(length) == length - 1).reshape((length, 1, 1, 1))
        shifted = jnp.where(at_edge, -shifted, shifted)
    if course == 1:
        at_edge = (jnp.arange(length) == length - 1).reshape((length, 1, 1))
        shifted = jnp.where(at_edge, jnp.flip(shifted, axis=field.ndim - 5), shifted)
    return shifted


def behind(field, course):
    axis_no = field.ndim + course - 4
    shifted = jnp.roll(field, 1, axis=axis_no)
    length = field.shape[axis_no]
    if course == 0:
        at_edge = (jnp.arange(length) == 0).reshape((length, 1, 1, 1))
        shifted = jnp.where(at_edge, -shifted, shifted)
    if course == 1:
        at_edge = (jnp.arange(length) == 0).reshape((length, 1, 1))
        shifted = jnp.where(at_edge, jnp.flip(shifted, axis=field.ndim - 5), shifted)
    return shifted


def apply_hop(spinor, link_re, link_im):
    summed = None
    for course in range(4):
        ahead_field = ahead(project_minus(spinor, course), course)
        plus_moved = color_apply(link_re[course], link_im[course], project_plus(spinor, course), True)
        behind_field = behind(plus_moved, course)
        contrib = rebuild_minus(color_apply(link_re[course], link_im[course], ahead_field, False), course) + rebuild_plus(behind_field, course)
        summed = contrib if summed is None else summed + contrib
    return summed


def run_series(start, link_re, link_im):
    values = start
    for sweep_index in range(DEGREE):
        values = start + hopping * apply_hop(values, link_re, link_im)
    return values


def reference(source, gauge_links, photon_angles):
    link_re, link_im = combine_links(gauge_links, photon_angles)
    forward_sol = run_series(source, link_re, link_im)
    adjoint_sol = gamma_five(run_series(gamma_five(forward_sol), link_re, link_im))
    force_re = []
    force_im = []
    photon_parts = []
    for course in range(4):
        ahead_x = ahead(project_minus(forward_sol, course), course)
        ahead_y = ahead(project_plus(adjoint_sol, course), course)
        here_y = project_minus(adjoint_sol, course)
        here_x = project_plus(forward_sol, course)
        first_re, first_im = outer_product(ahead_x, here_y)
        second_re, second_im = outer_product(ahead_y, here_x)
        anti_re, anti_im, photon_part = link_force(link_re[course], link_im[course], first_re + second_re, first_im + second_im)
        force_re.append(anti_re)
        force_im.append(anti_im)
        photon_parts.append(photon_part)
    color_force = jnp.stack([jnp.stack(force_re), jnp.stack(force_im)])
    photon_force = jnp.stack(photon_parts)
    return color_force, photon_force
```

```python
import functools

import jax
import jax.numpy as jnp
from jax import lax
from jax.experimental import pallas as pl
from jax.experimental.pallas import tpu as pltpu
from jax.sharding import PartitionSpec as P

DEGREE = 4
HOPPING = 0.15
CHARGE = 2.0 / 3.0
MESH = pl.DeviceIdType.MESH

A_MATRIX = (
    ((0, 2), (1, 2)),
    ((1, 3), (0, 3)),
    ((1, 2), (0, 0)),
    ((0, 3), (1, 1)),
)
A_DAGGER = (
    ((0, 2), (1, 2)),
    ((1, 1), (0, 1)),
    ((1, 0), (0, 2)),
    ((0, 1), (1, 3)),
)


def add_phase(u, w, phase):
    phase = phase % 4
    if phase == 0:
        return (u[0] + w[0], u[1] + w[1])
    if phase == 1:
        return (u[0] - w[1], u[1] + w[0])
    if phase == 2:
        return (u[0] - w[0], u[1] - w[1])
    return (u[0] + w[1], u[1] - w[0])


def project(spinor, mu, plus):
    extra = 0 if plus else 2
    half = []
    for s in range(2):
        k, phase = A_MATRIX[mu][s]
        half.append([add_phase(spinor[s][a], spinor[2 + k][a], phase + extra) for a in range(3)])
    return half


def accumulate(total, half, mu, plus):
    extra = 0 if plus else 2
    out = []
    for s in range(2):
        out.append([add_phase(total[s][a], half[s][a], 0) for a in range(3)])
    for s in range(2):
        k, phase = A_DAGGER[mu][s]
        out.append([add_phase(total[2 + s][a], half[k][a], phase + extra) for a in range(3)])
    return out


def color_apply(link, half, dagger):
    out = []
    for s in range(2):
        rows = []
        for a in range(3):
            re = im = None
            for b in range(3):
                hr, hi = half[s][b]
                if dagger:
                    lr, li = link[b][a]
                    tr, ti = lr * hr + li * hi, lr * hi - li * hr
                else:
                    lr, li = link[a][b]
                    tr, ti = lr * hr - li * hi, lr * hi + li * hr
                re = tr if re is None else re + tr
                im = ti if im is None else im + ti
            rows.append((re, im))
        out.append(rows)
    return out


def map_half(fn, half):
    return [[(fn(h[0]), fn(h[1])) for h in row] for row in half]


def load_spinor(ref, c, t):
    return [[(ref[0, s, a, c, t], ref[1, s, a, c, t]) for a in range(3)] for s in range(4)]


def store_spinor(ref, c, t, values):
    for s in range(4):
        for a in range(3):
            ref[0, s, a, c, t] = values[s][a][0]
            ref[1, s, a, c, t] = values[s][a][1]


def load_half(ref, *where):
    return [[(ref[(0, s, a) + where], ref[(1, s, a) + where]) for a in range(3)] for s in range(2)]


def store_half(ref, half, *where):
    for s in range(2):
        for a in range(3):
            ref[(0, s, a) + where] = half[s][a][0]
            ref[(1, s, a) + where] = half[s][a][1]


def kernel(sizes, src, links, angles, force, photon, L, S, V, PX, send, recv, fsend, frecv,
           send_sem, recv_sem, fsend_sem, frecv_sem):
    copies, nt, nx, ny, nz = sizes
    R = nx * ny
    axes = ("ta", "gx", "yz")
    count = [lax.axis_size(a) for a in axes]
    here = [lax.axis_index(a) for a in axes]
    lower = [lax.rem(here[k] + count[k] - 1, count[k]) for k in range(3)]
    upper = [lax.rem(here[k] + 1, count[k]) for k in range(3)]

    def device(k, index):
        return tuple(index if j == k else here[j] for j in range(3))

    barrier = pltpu.get_barrier_semaphore()
    for k in range(3):
        for index in (lower[k], upper[k]):
            pl.semaphore_signal(barrier, inc=1, device_id=device(k, index), device_id_type=MESH)

    first = [(count[k] - here[k]) // count[k] for k in range(3)]
    last = [(here[k] + 1) // count[k] for k in range(3)]
    sign_ahead = (1 - 2 * first[0]).astype(jnp.float32)
    sign_behind = (1 - 2 * last[0]).astype(jnp.float32)
    row = lax.broadcasted_iota(jnp.int32, (R, nz), 0)
    row_x = row // ny
    row_y = row % ny

    for mu in range(4):
        def combine(t, carry):
            angle = CHARGE * angles[mu, t]
            cosine = HOPPING * jnp.cos(angle)
            sine = HOPPING * jnp.sin(angle)
            for a in range(3):
                for b in range(3):
                    re = links[0, mu, a, b, t]
                    im = links[1, mu, a, b, t]
                    L[0, mu, a, b, t] = cosine * re - sine * im
                    L[1, mu, a, b, t] = cosine * im + sine * re
            return carry

        lax.fori_loop(0, nt, combine, 0)

    def load_link(mu, c, t):
        sign = (1 - 2 * c).astype(jnp.float32)
        return [[(L[0, mu, a, b, t], L[1, mu, a, b, t] * sign) for b in range(3)] for a in range(3)]

    def items(body, times=nt):
        def step(i, carry):
            body(i % copies, i // copies)
            return carry

        lax.fori_loop(0, times * copies, step, 0)

    for group in (send[2:], fsend[1:]):
        for ref in group:
            ref[...] = jnp.zeros_like(ref)

    def start_field(c, t):
        values = load_spinor(src, c, t)
        store_spinor(S, c, t, values)
        store_spinor(V.at[0], c, t, values)

    items(start_field)

    def copy_of(kind, parity):
        k = kind // 2
        to = lower[k] if kind % 2 == 0 else upper[k]
        return pltpu.make_async_remote_copy(
            src_ref=send[kind], dst_ref=recv[kind].at[parity],
            send_sem=send_sem.at[kind], recv_sem=recv_sem.at[kind, parity],
            device_id=device(k, to), device_id_type=MESH)

    def force_copy(k):
        return pltpu.make_async_remote_copy(
            src_ref=fsend[k], dst_ref=frecv[k],
            send_sem=fsend_sem.at[k], recv_sem=frecv_sem.at[k],
            device_id=device(k, lower[k]), device_id_type=MESH)

    def slot_of(k, c, t, flip):
        if k == 1:
            i = t * copies + c + flip * (1 - 2 * c)
            return i // nx, i % nx
        i = t * copies + c
        return i // ny, i % ny

    def pack(ref, half, k, c, t, ahead):
        if k == 1:
            tile, slot = slot_of(1, c, t, first[1] if ahead else last[1])
            shift = slot * ny if ahead else (slot + 1) * ny
            mask = row_x == slot
        else:
            tile, slot = slot_of(2, c, t, 0)
            shift = slot if ahead else slot + 1 + R - ny
            mask = row_y == slot
        shift = lax.rem(shift, R)
        for s in range(2):
            for a in range(3):
                for ri in range(2):
                    moved = pltpu.roll(half[s][a][ri], shift, 0)
                    ref[ri, s, a, tile] = jnp.where(mask, moved, ref[ri, s, a, tile])

    def shifted(half, ref, k, c, t, ahead):
        tile, slot = slot_of(k, c, t, 0)
        if k == 1:
            own = R - ny if ahead else ny
            shift = (nx - 1 - slot) * ny if ahead else (nx - slot) * ny
            mask = row_x == (nx - 1 if ahead else 0)
        else:
            own = R - 1 if ahead else 1
            shift = ny - 1 - slot if ahead else R - slot
            mask = row_y == (ny - 1 if ahead else 0)
        shift = lax.rem(shift, R)
        out = []
        for s in range(2):
            line = []
            for a in range(3):
                line.append(tuple(
                    jnp.where(mask, pltpu.roll(ref[ri, s, a, tile], shift, 0),
                              pltpu.roll(half[s][a][ri], own, 0))
                    for ri in range(2)))
            out.append(line)
        return out

    def ahead_face_t(field, ref, plus):
        def body(c, t):
            half = project(load_spinor(field, c, 0), 0, plus)
            store_half(ref, map_half(lambda h: h * sign_ahead, half), c)
        items(body, 1)

    def z_ahead(half):
        return map_half(lambda h: pltpu.roll(h, nz - 1, 1), half)

    def z_behind(half):
        return map_half(lambda h: pltpu.roll(h, 1, 1), half)

    pl.semaphore_wait(barrier, 6)

    def hop(n, carry):
        parity = lax.rem(n, 2)
        now = V.at[parity]
        new = V.at[1 - parity]

        @pl.when(n == DEGREE)
        def _():
            def restart(c, t):
                values = load_spinor(now, c, t)
                values = values[:2] + map_half(lambda h: -h, values[2:])
                store_spinor(S, c, t, values)
                store_spinor(now, c, t, values)
            items(restart)

        def face_t(c, t):
            half = project(load_spinor(now, c, 0), 0, False)
            store_half(send[0], map_half(lambda h: h * sign_ahead, half), c)
            half = project(load_spinor(now, c, nt - 1), 0, True)
            half = color_apply(load_link(0, c, nt - 1), half, True)
            store_half(send[1], map_half(lambda h: h * sign_behind, half), c)

        items(face_t, 1)
        copy_of(0, parity).start()
        copy_of(1, parity).start()

        def face_xy(c, t):
            spinor = load_spinor(now, c, t)
            for k in (1, 2):
                pack(send[2 * k], project(spinor, k, False), k, c, t, True)
                half = color_apply(load_link(k, c, t), project(spinor, k, True), True)
                store_half(PX.at[k - 1], half, c, t)
                pack(send[2 * k + 1], half, k, c, t, False)

        items(face_xy)
        for kind in range(2, 6):
            copy_of(kind, parity).start()

        @pl.when(n == DEGREE)
        def _():
            ahead_face_t(S, fsend[0], True)

            def face(c, t):
                spinor = load_spinor(S, c, t)
                for k in (1, 2):
                    pack(fsend[k], project(spinor, k, True), k, c, t, True)
            items(face)
            for k in range(3):
                force_copy(k).start()

        def along_z(c, t):
            total = load_spinor(S, c, t)
            spinor = load_spinor(now, c, t)
            link = load_link(3, c, t)
            half = color_apply(link, project(spinor, 3, True), True)
            total = accumulate(total, z_behind(half), 3, True)
            half = color_apply(link, z_ahead(project(spinor, 3, False)), False)
            total = accumulate(total, half, 3, False)
            store_spinor(new, c, t, total)

        items(along_z)

        def along_t(c, t):
            link = load_link(0, c, t)
            half = color_apply(link, project(load_spinor(now, c, t + 1), 0, False), False)
            store_spinor(new, c, t, accumulate(load_spinor(new, c, t), half, 0, False))
            half = color_apply(link, project(load_spinor(now, c, t), 0, True), True)
            store_spinor(new, c, t + 1, accumulate(load_spinor(new, c, t + 1), half, 0, True))

        if nt > 1:
            items(along_t, nt - 1)

        for kind in range(2, 6):
            copy_of(kind, parity).wait_recv()

        def along_xy(c, t):
            spinor = load_spinor(now, c, t)
            total = load_spinor(new, c, t)
            for k in (1, 2):
                half = shifted(project(spinor, k, False), recv[2 * k].at[parity], k, c, t, True)
                half = color_apply(load_link(k, c, t), half, False)
                total = accumulate(total, half, k, False)
                half = load_half(PX.at[k - 1], c, t)
                half = shifted(half, recv[2 * k + 1].at[parity], k, c, t, False)
                total = accumulate(total, half, k, True)
            store_spinor(new, c, t, total)

        items(along_xy)

        for kind in range(2):
            copy_of(kind, parity).wait_recv()

        def edge_t(c, t):
            half = load_half(recv[0].at[parity], c)
            half = color_apply(load_link(0, c, nt - 1), half, False)
            total = load_spinor(new, c, nt - 1)
            store_spinor(new, c, nt - 1, accumulate(total, half, 0, False))
            half = load_half(recv[1].at[parity], c)
            store_spinor(new, c, 0, accumulate(load_spinor(new, c, 0), half, 0, True))

        items(edge_t, 1)
        for kind in range(6):
            copy_of(kind, parity).wait_send()
        return carry

    lax.fori_loop(0, 2 * DEGREE, hop, 0)

    W = V.at[0]
    ahead_face_t(W, send[0], False)
    copy_of(0, 0).start()

    def last_face(c, t):
        spinor = load_spinor(W, c, t)
        for k in (1, 2):
            pack(send[2 * k], project(spinor, k, False), k, c, t, True)

    items(last_face)
    copy_of(2, 0).start()
    copy_of(4, 0).start()

    def outer_into(out, left, right):
        for a in range(3):
            for b in range(3):
                for s in range(2):
                    lr, li = left[s][a]
                    rr, ri = right[s][b]
                    re = lr * rr + li * ri
                    im = li * rr - lr * ri
                    old = out[a][b]
                    out[a][b] = (re, im) if old is None else (old[0] + re, old[1] + im)
        return out

    def finish(mu, t, heads):
        both = None
        for c in range(copies):
            ahead_x, ahead_y = heads(c)
            here_y = project(load_spinor(W, c, t), mu, True)
            here_x = project(load_spinor(S, c, t), mu, False)
            out = [[None] * 3 for _ in range(3)]
            out = outer_into(out, ahead_x, here_y)
            out = outer_into(out, ahead_y, here_x)
            if both is None:
                both = out
            else:
                both = [[(both[a][b][0] + out[a][b][0], both[a][b][1] - out[a][b][1])
                         for b in range(3)] for a in range(3)]
        merged = []
        for a in range(3):
            line = []
            for b in range(3):
                re = im = None
                for k in range(3):
                    lr, li = L[0, mu, a, k, t], L[1, mu, a, k, t]
                    br, bi = both[k][b]
                    tr, ti = lr * br - li * bi, lr * bi + li * br
                    re = tr if re is None else re + tr
                    im = ti if im is None else im + ti
                line.append((re, im))
            merged.append(line)
        trace = merged[0][0][1] + merged[1][1][1] + merged[2][2][1]
        third = trace * (1.0 / 3.0)
        photon[mu, t] = CHARGE * trace
        for a in range(3):
            force[0, mu, a, a, t] = jnp.zeros_like(trace)
            force[1, mu, a, a, t] = merged[a][a][1] - third
            for b in range(a + 1, 3):
                re = 0.5 * (merged[a][b][0] - merged[b][a][0])
                im = 0.5 * (merged[a][b][1] + merged[b][a][1])
                force[0, mu, a, b, t] = re
                force[0, mu, b, a, t] = -re
                force[1, mu, a, b, t] = im
                force[1, mu, b, a, t] = im

    def over_t(body, times=nt):
        def step(t, carry):
            body(t)
            return carry
        lax.fori_loop(0, times, step, 0)

    def force_z(t):
        finish(3, t, lambda c: (z_ahead(project(load_spinor(S, c, t), 3, True)),
                                z_ahead(project(load_spinor(W, c, t), 3, False))))

    over_t(force_z)

    def force_t(t):
        finish(0, t, lambda c: (project(load_spinor(S, c, t + 1), 0, True),
                                project(load_spinor(W, c, t + 1), 0, False)))

    if nt > 1:
        over_t(force_t, nt - 1)

    for k in (2, 1, 0):
        force_copy(k).wait()
        copy_of(2 * k, 0).wait()
        if k == 0:
            finish(0, nt - 1, lambda c: (load_half(frecv[0], c), load_half(recv[0].at[0], c)))
        else:
            def force_k(t):
                finish(k, t, lambda c: (
                    shifted(project(load_spinor(S, c, t), k, True), frecv[k], k, c, t, True),
                    shifted(project(load_spinor(W, c, t), k, False), recv[2 * k].at[0], k, c, t,
                            True)))
            over_t(force_k)


def per_device(source, gauge_links, photon_angles):
    _, _, _, copies, nt, nx, ny, nz = source.shape
    R = nx * ny
    total = copies * nt
    face = [(2, 2, 3, copies, R, nz),
            (2, 2, 3, -(-total // nx), R, nz),
            (2, 2, 3, -(-total // ny), R, nz)]
    f32 = jnp.float32
    field = (2, 4, 3, copies, nt, R, nz)

    def vm(shape):
        return pltpu.VMEM(shape, f32)

    color, photon = pl.pallas_call(
        functools.partial(kernel, (copies, nt, nx, ny, nz)),
        out_shape=(jax.ShapeDtypeStruct((2, 4, 3, 3, nt, R, nz), f32),
                   jax.ShapeDtypeStruct((4, nt, R, nz), f32)),
        in_specs=[pl.BlockSpec(memory_space=pltpu.VMEM)] * 3,
        out_specs=(pl.BlockSpec(memory_space=pltpu.VMEM),) * 2,
        scratch_shapes=[
            vm((2, 4, 3, 3, nt, R, nz)),
            vm(field),
            vm((2,) + field),
            vm((2, 2, 2, 3, copies, nt, R, nz)),
            [vm(face[kind // 2]) for kind in range(6)],
            [vm((2,) + face[kind // 2]) for kind in range(6)],
            [vm(face[k]) for k in range(3)],
            [vm(face[k]) for k in range(3)],
            pltpu.SemaphoreType.DMA((6,)),
            pltpu.SemaphoreType.DMA((6, 2)),
            pltpu.SemaphoreType.DMA((3,)),
            pltpu.SemaphoreType.DMA((3,)),
        ],
        compiler_params=pltpu.CompilerParams(
            collective_id=0, has_side_effects=True, vmem_limit_bytes=40 * 1024 * 1024),
    )(source.reshape(2, 4, 3, copies, nt, R, nz),
      gauge_links.reshape(2, 4, 3, 3, nt, R, nz),
      photon_angles.reshape(4, nt, R, nz))
    return (color.reshape(2, 4, 3, 3, nt, nx, ny, nz), photon.reshape(4, nt, nx, ny, nz))


def solution(mesh):
    in_specs = (
        P(None, None, None, None, "ta", "gx", "yz", None),
        P(None, None, None, None, "ta", "gx", "yz", None),
        P(None, "ta", "gx", "yz", None),
    )
    out_specs = (P(None, None, None, None, "ta", "gx", "yz", None), P(None, "ta", "gx", "yz", None))
    return jax.shard_map(
        per_device, mesh=mesh, in_specs=in_specs, out_specs=out_specs, check_vma=False
    )
```

```python
import functools

import jax
import jax.numpy as jnp
from jax import lax
from jax.experimental import pallas as pl
from jax.experimental.pallas import tpu as pltpu
from jax.sharding import PartitionSpec as P

DEGREE = 4
HOPPING = 0.15
CHARGE = 2.0 / 3.0
MESH = pl.DeviceIdType.MESH

A_MATRIX = (
    ((0, 2), (1, 2)),
    ((1, 3), (0, 3)),
    ((1, 2), (0, 0)),
    ((0, 3), (1, 1)),
)
A_DAGGER = (
    ((0, 2), (1, 2)),
    ((1, 1), (0, 1)),
    ((1, 0), (0, 2)),
    ((0, 1), (1, 3)),
)


def add_phase(u, w, phase):
    phase = phase % 4
    if phase == 0:
        return (u[0] + w[0], u[1] + w[1])
    if phase == 1:
        return (u[0] - w[1], u[1] + w[0])
    if phase == 2:
        return (u[0] - w[0], u[1] - w[1])
    return (u[0] + w[1], u[1] - w[0])


def project(spinor, mu, plus):
    extra = 0 if plus else 2
    half = []
    for s in range(2):
        k, phase = A_MATRIX[mu][s]
        half.append([add_phase(spinor[s][a], spinor[2 + k][a], phase + extra) for a in range(3)])
    return half


def accumulate(total, half, mu, plus):
    extra = 0 if plus else 2
    out = []
    for s in range(2):
        out.append([add_phase(total[s][a], half[s][a], 0) for a in range(3)])
    for s in range(2):
        k, phase = A_DAGGER[mu][s]
        out.append([add_phase(total[2 + s][a], half[k][a], phase + extra) for a in range(3)])
    return out


def color_apply(link, half, dagger):
    out = []
    for s in range(2):
        rows = []
        for a in range(3):
            re = im = None
            for b in range(3):
                hr, hi = half[s][b]
                if dagger:
                    lr, li = link[b][a]
                    tr, ti = lr * hr + li * hi, lr * hi - li * hr
                else:
                    lr, li = link[a][b]
                    tr, ti = lr * hr - li * hi, lr * hi + li * hr
                re = tr if re is None else re + tr
                im = ti if im is None else im + ti
            rows.append((re, im))
        out.append(rows)
    return out


def map_half(fn, half):
    return [[(fn(h[0]), fn(h[1])) for h in row] for row in half]


def load_spinor(ref, t):
    return [[(ref[0, s, a, t], ref[1, s, a, t]) for a in range(3)] for s in range(4)]


def store_spinor(ref, t, values):
    for s in range(4):
        for a in range(3):
            ref[0, s, a, t] = values[s][a][0]
            ref[1, s, a, t] = values[s][a][1]


def load_half(ref, *where):
    return [[(ref[(0, s, a) + where], ref[(1, s, a) + where]) for a in range(3)] for s in range(2)]


def store_half(ref, half, *where):
    for s in range(2):
        for a in range(3):
            ref[(0, s, a) + where] = half[s][a][0]
            ref[(1, s, a) + where] = half[s][a][1]


def kernel(sizes, src, links, angles, force, photon, L, S, V, PX, send, recv, fsend, frecv,
           send_sem, recv_sem, fsend_sem, frecv_sem):
    copies, nt, nx, ny, nz = sizes
    R = nx * ny
    axes = ("ta", "gx", "yz")
    count = [lax.axis_size(a) for a in axes]
    here = [lax.axis_index(a) for a in axes]
    lower = [lax.rem(here[k] + count[k] - 1, count[k]) for k in range(3)]
    upper = [lax.rem(here[k] + 1, count[k]) for k in range(3)]

    def device(k, index):
        return tuple(index if j == k else here[j] for j in range(3))

    barrier = pltpu.get_barrier_semaphore()
    for k in range(3):
        for index in (lower[k], upper[k]):
            pl.semaphore_signal(barrier, inc=1, device_id=device(k, index), device_id_type=MESH)

    first = [(count[k] - here[k]) // count[k] for k in range(3)]
    last = [(here[k] + 1) // count[k] for k in range(3)]
    sign_ahead = (1 - 2 * first[0]).astype(jnp.float32)
    sign_behind = (1 - 2 * last[0]).astype(jnp.float32)
    row = lax.broadcasted_iota(jnp.int32, (R, nz), 0)
    row_x = row // ny
    row_y = row % ny

    lane = lax.broadcasted_iota(jnp.int32, (R, nz), 1)
    corner = here[0] * nt + here[1] * nx + here[2] * ny

    def even(t):
        return (corner + t + row_x + row_y + lane) % 2 == 0

    def merge(t, zero, one, p):
        mask = even(t)
        if p == 0:
            return jnp.where(mask, zero, one)
        return jnp.where(mask, one, zero)

    def over_t(body, times=nt):
        def step(t, carry):
            body(t)
            return carry

        lax.fori_loop(0, times, step, 0)

    for mu in range(4):
        def combine(t):
            angle = CHARGE * angles[mu, t]
            cosine = HOPPING * jnp.cos(angle)
            sine = HOPPING * jnp.sin(angle)
            for a in range(3):
                for b in range(3):
                    re = links[0, mu, a, b, t]
                    im = links[1, mu, a, b, t]
                    re, im = cosine * re - sine * im, cosine * im + sine * re
                    re_one, im_one = pltpu.roll(re, nz - 1, 1), -pltpu.roll(im, nz - 1, 1)
                    for p in range(2):
                        L[p, 0, mu, a, b, t] = merge(t, re, re_one, p)
                        L[p, 1, mu, a, b, t] = merge(t, im, im_one, p)

        over_t(combine)

    def load_link(p, mu, t):
        return [[(L[p, 0, mu, a, b, t], L[p, 1, mu, a, b, t]) for b in range(3)] for a in range(3)]

    for group in (send[2:], fsend[1:]):
        for ref in group:
            ref[...] = jnp.zeros_like(ref)

    def start_field(t):
        for s in range(4):
            for a in range(3):
                for ri in range(2):
                    zero = src[ri, s, a, 0, t]
                    one = pltpu.roll(src[ri, s, a, 1, t], nz - 1, 1)
                    for p in range(2):
                        value = merge(t, zero, one, p)
                        S[p, ri, s, a, t] = value
                        V[0, p, ri, s, a, t] = value

    over_t(start_field)

    def copy_of(kind, m):
        k = kind // 2
        to = lower[k] if kind % 2 == 0 else upper[k]
        chain, slot = lax.rem(m, 2), lax.rem(m, 4)
        return pltpu.make_async_remote_copy(
            src_ref=send[kind].at[chain], dst_ref=recv[kind].at[slot],
            send_sem=send_sem.at[kind, chain], recv_sem=recv_sem.at[kind, slot],
            device_id=device(k, to), device_id_type=MESH)

    def force_copy(k, p):
        return pltpu.make_async_remote_copy(
            src_ref=fsend[k].at[p], dst_ref=frecv[k].at[p],
            send_sem=fsend_sem.at[k, p], recv_sem=frecv_sem.at[k, p],
            device_id=device(k, lower[k]), device_id_type=MESH)

    def slot_of(k, ri, t):
        i = ri * nt + t
        return (i // nx, i % nx) if k == 1 else (i // ny, i % ny)

    def pack(ref, half, k, t, ahead):
        for ri in range(2):
            tile, slot = slot_of(k, ri, t)
            if k == 1:
                shift = slot * ny if ahead else (slot + 1) * ny
                mask = row_x == slot
            else:
                shift = slot if ahead else slot + 1 + R - ny
                mask = row_y == slot
            shift = lax.rem(shift, R)
            for s in range(2):
                for a in range(3):
                    moved = pltpu.roll(half[s][a][ri], shift, 0)
                    ref[s, a, tile] = jnp.where(mask, moved, ref[s, a, tile])

    def shifted(half, ref, k, p, t, ahead):
        out = [[[None, None] for a in range(3)] for s in range(2)]
        if k == 1:
            own = R - ny if ahead else ny
            mask = row_x == (nx - 1 if ahead else 0)
            wraps = (last[1] if ahead else first[1]) == 1
            copy_zero = (corner + t + row_x + row_y + lane + p) % 2 == 0
        else:
            own = R - 1 if ahead else 1
            mask = row_y == (ny - 1 if ahead else 0)
        for ri in range(2):
            tile, slot = slot_of(k, ri, t)
            if k == 1:
                shift = (nx - 1 - slot) * ny if ahead else (nx - slot) * ny
            else:
                shift = ny - 1 - slot if ahead else R - slot
            shift = lax.rem(shift, R)
            for s in range(2):
                for a in range(3):
                    face = pltpu.roll(ref[s, a, tile], shift, 0)
                    if k == 1:
                        other = jnp.where(copy_zero, pltpu.roll(face, 1, 1),
                                          pltpu.roll(face, nz - 1, 1))
                        face = jnp.where(wraps, other, face)
                    out[s][a][ri] = jnp.where(mask, face, pltpu.roll(half[s][a][ri], own, 0))
        return out

    def z_ahead(half):
        return map_half(lambda h: pltpu.roll(h, nz - 1, 1), half)

    def z_behind(half):
        return map_half(lambda h: pltpu.roll(h, 1, 1), half)

    def ahead_face_t(field, ref, plus):
        half = project(load_spinor(field, 0), 0, plus)
        store_half(ref, map_half(lambda h: h * sign_ahead, half))

    def send_faces(field, p, m, behind):
        chain = lax.rem(m, 2)
        ahead_face_t(field, send[0].at[chain], False)
        copy_of(0, m).start()

        def behind_t():
            half = project(load_spinor(field, nt - 1), 0, True)
            half = color_apply(load_link(p, 0, nt - 1), half, True)
            store_half(send[1].at[chain], map_half(lambda h: h * sign_behind, half))
            copy_of(1, m).start()

        pl.when(behind)(behind_t)

        def face_xy(t):
            spinor = load_spinor(field, t)
            for k in (1, 2):
                pack(send[2 * k].at[chain], project(spinor, k, False), k, t, True)
                half = color_apply(load_link(p, k, t), project(spinor, k, True), True)
                store_half(PX.at[chain, k - 1], half, t)
                pack(send[2 * k + 1].at[chain], half, k, t, False)

        over_t(face_xy)
        copy_of(2, m).start()
        copy_of(4, m).start()

        def behind_xy():
            copy_of(3, m).start()
            copy_of(5, m).start()

        pl.when(behind)(behind_xy)

    rounds = 2 * DEGREE
    pl.semaphore_wait(barrier, 6)

    def first_faces(m, carry):
        send_faces(V.at[0, m], m, m, m >= 0)
        return carry

    lax.fori_loop(0, 2, first_faces, 0)

    def hop(m, carry):
        n = m // 2
        chain = lax.rem(m, 2)
        slot = lax.rem(m, 4)
        p = lax.rem(chain + n, 2)
        q = 1 - p
        now = V.at[lax.rem(n, 2), p]
        new = V.at[lax.rem(n + 1, 2), q]

        def along_z(t):
            total = load_spinor(S.at[q], t)
            spinor = load_spinor(now, t)
            half = color_apply(load_link(p, 3, t), project(spinor, 3, True), True)
            total = accumulate(total, z_behind(half), 3, True)
            half = z_ahead(project(spinor, 3, False))
            half = color_apply(load_link(q, 3, t), half, False)
            total = accumulate(total, half, 3, False)
            store_spinor(new, t, total)

        over_t(along_z)

        def along_t(t):
            half = project(load_spinor(now, t + 1), 0, False)
            half = color_apply(load_link(q, 0, t), half, False)
            store_spinor(new, t, accumulate(load_spinor(new, t), half, 0, False))
            half = color_apply(load_link(p, 0, t), project(load_spinor(now, t), 0, True), True)
            store_spinor(new, t + 1, accumulate(load_spinor(new, t + 1), half, 0, True))

        if nt > 1:
            over_t(along_t, nt - 1)

        for kind in range(2, 6):
            copy_of(kind, m).wait_recv()

        def along_xy(t):
            spinor = load_spinor(now, t)
            total = load_spinor(new, t)
            for k in (1, 2):
                half = shifted(project(spinor, k, False), recv[2 * k].at[slot], k, q, t, True)
                half = color_apply(load_link(q, k, t), half, False)
                total = accumulate(total, half, k, False)
                half = load_half(PX.at[chain, k - 1], t)
                half = shifted(half, recv[2 * k + 1].at[slot], k, q, t, False)
                total = accumulate(total, half, k, True)
            store_spinor(new, t, total)

        over_t(along_xy)

        for kind in range(2):
            copy_of(kind, m).wait_recv()
        half = color_apply(load_link(q, 0, nt - 1), load_half(recv[0].at[slot]), False)
        total = accumulate(load_spinor(new, nt - 1), half, 0, False)
        store_spinor(new, nt - 1, total)
        half = load_half(recv[1].at[slot])
        store_spinor(new, 0, accumulate(load_spinor(new, 0), half, 0, True))
        for kind in range(6):
            copy_of(kind, m).wait_send()

        @pl.when(n == DEGREE - 1)
        def _():
            def restart(t):
                values = load_spinor(new, t)
                values = values[:2] + map_half(lambda h: -h, values[2:])
                store_spinor(S.at[q], t, values)
                store_spinor(new, t, values)

            over_t(restart)

        send_faces(new, q, m + 2, n < rounds - 1)

        @pl.when(n == DEGREE - 1)
        def _():
            ahead_face_t(S.at[q], fsend[0].at[q], True)

            def face(t):
                spinor = load_spinor(S.at[q], t)
                for k in (1, 2):
                    pack(fsend[k].at[q], project(spinor, k, True), k, t, True)

            over_t(face)
            for k in range(3):
                force_copy(k, q).start()

        return carry

    lax.fori_loop(0, 2 * rounds, hop, 0)

    W = V.at[rounds % 2]

    def outer_into(out, left, right):
        for a in range(3):
            for b in range(3):
                for s in range(2):
                    lr, li = left[s][a]
                    rr, ri = right[s][b]
                    re = lr * rr + li * ri
                    im = li * rr - lr * ri
                    old = out[a][b]
                    out[a][b] = (re, im) if old is None else (old[0] + re, old[1] + im)
        return out

    def finish(mu, t, heads):
        parts = []
        for q in range(2):
            ahead_x, ahead_y = heads(1 - q)
            here_y = project(load_spinor(W.at[q], t), mu, True)
            here_x = project(load_spinor(S.at[q], t), mu, False)
            out = [[None] * 3 for _ in range(3)]
            out = outer_into(out, ahead_x, here_y)
            parts.append(outer_into(out, ahead_y, here_x))
        both, link = [], []
        for a in range(3):
            line, link_line = [], []
            for b in range(3):
                pair, link_pair = [], []
                for ri in range(2):
                    zero, one = parts[0][a][b][ri], parts[1][a][b][ri]
                    copy_one = pltpu.roll(merge(t, zero, one, 1), 1, 1)
                    copy_zero = merge(t, zero, one, 0)
                    pair.append(copy_zero + copy_one if ri == 0 else copy_zero - copy_one)
                    link_pair.append(merge(t, L[0, ri, mu, a, b, t], L[1, ri, mu, a, b, t], 0))
                line.append(pair)
                link_line.append(link_pair)
            both.append(line)
            link.append(link_line)
        merged = []
        for a in range(3):
            line = []
            for b in range(3):
                re = im = None
                for k in range(3):
                    lr, li = link[a][k]
                    br, bi = both[k][b]
                    tr, ti = lr * br - li * bi, lr * bi + li * br
                    re = tr if re is None else re + tr
                    im = ti if im is None else im + ti
                line.append((re, im))
            merged.append(line)
        trace = merged[0][0][1] + merged[1][1][1] + merged[2][2][1]
        third = trace * (1.0 / 3.0)
        photon[mu, t] = CHARGE * trace
        for a in range(3):
            force[0, mu, a, a, t] = jnp.zeros_like(trace)
            force[1, mu, a, a, t] = merged[a][a][1] - third
            for b in range(a + 1, 3):
                re = 0.5 * (merged[a][b][0] - merged[b][a][0])
                im = 0.5 * (merged[a][b][1] + merged[b][a][1])
                force[0, mu, a, b, t] = re
                force[0, mu, b, a, t] = -re
                force[1, mu, a, b, t] = im
                force[1, mu, b, a, t] = im

    def force_z(t):
        finish(3, t, lambda p: (z_ahead(project(load_spinor(S.at[p], t), 3, True)),
                                z_ahead(project(load_spinor(W.at[p], t), 3, False))))

    over_t(force_z)

    def force_t(t):
        finish(0, t, lambda p: (project(load_spinor(S.at[p], t + 1), 0, True),
                                project(load_spinor(W.at[p], t + 1), 0, False)))

    if nt > 1:
        over_t(force_t, nt - 1)

    numbers = [2 * rounds + (p + rounds) % 2 for p in range(2)]
    for k in (2, 1, 0):
        for p in range(2):
            force_copy(k, p).wait()
            copy_of(2 * k, numbers[p]).wait()
        if k == 0:
            finish(0, nt - 1, lambda p: (load_half(frecv[0].at[p]),
                                         load_half(recv[0].at[numbers[p] % 4])))
        else:
            def force_k(t):
                finish(k, t, lambda p: (
                    shifted(project(load_spinor(S.at[p], t), k, True), frecv[k].at[p],
                            k, 1 - p, t, True),
                    shifted(project(load_spinor(W.at[p], t), k, False),
                            recv[2 * k].at[numbers[p] % 4], k, 1 - p, t, True)))
            over_t(force_k)


def per_device(source, gauge_links, photon_angles):
    _, _, _, copies, nt, nx, ny, nz = source.shape
    R = nx * ny
    face = [(2, 2, 3, R, nz),
            (2, 3, -(-2 * nt // nx), R, nz),
            (2, 3, -(-2 * nt // ny), R, nz)]
    f32 = jnp.float32
    field = (2, 2, 4, 3, nt, R, nz)

    def vm(shape):
        return pltpu.VMEM(shape, f32)

    color, photon = pl.pallas_call(
        functools.partial(kernel, (copies, nt, nx, ny, nz)),
        out_shape=(jax.ShapeDtypeStruct((2, 4, 3, 3, nt, R, nz), f32),
                   jax.ShapeDtypeStruct((4, nt, R, nz), f32)),
        in_specs=[pl.BlockSpec(memory_space=pltpu.VMEM)] * 3,
        out_specs=(pl.BlockSpec(memory_space=pltpu.VMEM),) * 2,
        scratch_shapes=[
            vm((2, 2, 4, 3, 3, nt, R, nz)),
            vm(field),
            vm((2,) + field),
            vm((2, 2, 2, 2, 3, nt, R, nz)),
            [vm((2,) + face[kind // 2]) for kind in range(6)],
            [vm((4,) + face[kind // 2]) for kind in range(6)],
            [vm((2,) + face[k]) for k in range(3)],
            [vm((2,) + face[k]) for k in range(3)],
            pltpu.SemaphoreType.DMA((6, 2)),
            pltpu.SemaphoreType.DMA((6, 4)),
            pltpu.SemaphoreType.DMA((3, 2)),
            pltpu.SemaphoreType.DMA((3, 2)),
        ],
        compiler_params=pltpu.CompilerParams(
            collective_id=0, has_side_effects=True, vmem_limit_bytes=40 * 1024 * 1024),
    )(source.reshape(2, 4, 3, copies, nt, R, nz),
      gauge_links.reshape(2, 4, 3, 3, nt, R, nz),
      photon_angles.reshape(4, nt, R, nz))
    return (color.reshape(2, 4, 3, 3, nt, nx, ny, nz), photon.reshape(4, nt, nx, ny, nz))


def solution(mesh):
    in_specs = (
        P(None, None, None, None, "ta", "gx", "yz", None),
        P(None, None, None, None, "ta", "gx", "yz", None),
        P(None, "ta", "gx", "yz", None),
    )
    out_specs = (P(None, None, None, None, "ta", "gx", "yz", None), P(None, "ta", "gx", "yz", None))
    return jax.shard_map(
        per_device, mesh=mesh, in_specs=in_specs, out_specs=out_specs, check_vma=False
    )
```

```python
import functools

import jax
import jax.numpy as jnp
from jax import lax
from jax.experimental import pallas as pl
from jax.experimental.pallas import tpu as pltpu
from jax.sharding import PartitionSpec as P

DEGREE = 4
HOPPING = 0.15
CHARGE = 2.0 / 3.0
MESH = pl.DeviceIdType.MESH

A_MATRIX = (
    ((0, 2), (1, 2)),
    ((1, 3), (0, 3)),
    ((1, 2), (0, 0)),
    ((0, 3), (1, 1)),
)
A_DAGGER = (
    ((0, 2), (1, 2)),
    ((1, 1), (0, 1)),
    ((1, 0), (0, 2)),
    ((0, 1), (1, 3)),
)


def add_phase(u, w, phase):
    phase = phase % 4
    if phase == 0:
        return (u[0] + w[0], u[1] + w[1])
    if phase == 1:
        return (u[0] - w[1], u[1] + w[0])
    if phase == 2:
        return (u[0] - w[0], u[1] - w[1])
    return (u[0] + w[1], u[1] - w[0])


def project(spinor, mu, plus):
    extra = 0 if plus else 2
    half = []
    for s in range(2):
        k, phase = A_MATRIX[mu][s]
        half.append([add_phase(spinor[s][a], spinor[2 + k][a], phase + extra) for a in range(3)])
    return half


def accumulate(total, half, mu, plus):
    extra = 0 if plus else 2
    out = []
    for s in range(2):
        out.append([add_phase(total[s][a], half[s][a], 0) for a in range(3)])
    for s in range(2):
        k, phase = A_DAGGER[mu][s]
        out.append([add_phase(total[2 + s][a], half[k][a], phase + extra) for a in range(3)])
    return out


def color_apply(link, half, dagger):
    out = []
    for s in range(2):
        rows = []
        for a in range(3):
            re = im = None
            for b in range(3):
                hr, hi = half[s][b]
                if dagger:
                    lr, li = link[b][a]
                    tr, ti = lr * hr + li * hi, lr * hi - li * hr
                else:
                    lr, li = link[a][b]
                    tr, ti = lr * hr - li * hi, lr * hi + li * hr
                re = tr if re is None else re + tr
                im = ti if im is None else im + ti
            rows.append((re, im))
        out.append(rows)
    return out


def map_half(fn, half):
    return [[(fn(h[0]), fn(h[1])) for h in row] for row in half]


def load_spinor(ref, t):
    return [[(ref[0, s, a, t], ref[1, s, a, t]) for a in range(3)] for s in range(4)]


def store_spinor(ref, t, values):
    for s in range(4):
        for a in range(3):
            ref[0, s, a, t] = values[s][a][0]
            ref[1, s, a, t] = values[s][a][1]


def load_half(ref, *where):
    return [[(ref[(0, s, a) + where], ref[(1, s, a) + where]) for a in range(3)] for s in range(2)]


def store_half(ref, half, *where):
    for s in range(2):
        for a in range(3):
            ref[(0, s, a) + where] = half[s][a][0]
            ref[(1, s, a) + where] = half[s][a][1]


def kernel(sizes, src, links, angles, force, photon, L, S, V, PX, send, recv, fsend, frecv,
           send_sem, recv_sem, fsend_sem, frecv_sem):
    copies, nt, nx, ny, nz = sizes
    R = nx * ny
    axes = ("ta", "gx", "yz")
    count = [lax.axis_size(a) for a in axes]
    here = [lax.axis_index(a) for a in axes]
    lower = [lax.rem(here[k] + count[k] - 1, count[k]) for k in range(3)]
    upper = [lax.rem(here[k] + 1, count[k]) for k in range(3)]

    def device(k, index):
        return tuple(index if j == k else here[j] for j in range(3))

    barrier = pltpu.get_barrier_semaphore()
    for k in range(3):
        for index in (lower[k], upper[k]):
            pl.semaphore_signal(barrier, inc=1, device_id=device(k, index), device_id_type=MESH)

    first = [(count[k] - here[k]) // count[k] for k in range(3)]
    last = [(here[k] + 1) // count[k] for k in range(3)]
    sign_ahead = (1 - 2 * first[0]).astype(jnp.float32)
    sign_behind = (1 - 2 * last[0]).astype(jnp.float32)
    row = lax.broadcasted_iota(jnp.int32, (R, nz), 0)
    row_x = row // ny
    row_y = row % ny

    lane = lax.broadcasted_iota(jnp.int32, (R, nz), 1)
    corner = here[0] * nt + here[1] * nx + here[2] * ny

    def even(t):
        return (corner + t + row_x + row_y + lane) % 2 == 0

    def merge(t, zero, one, p):
        mask = even(t)
        if p == 0:
            return jnp.where(mask, zero, one)
        return jnp.where(mask, one, zero)

    def over_t(body, times=nt):
        def step(t, carry):
            body(t)
            return carry

        lax.fori_loop(0, times, step, 0)

    for mu in range(4):
        def combine(t):
            angle = CHARGE * angles[mu, t]
            cosine = HOPPING * jnp.cos(angle)
            sine = HOPPING * jnp.sin(angle)
            for a in range(3):
                for b in range(3):
                    re = links[0, mu, a, b, t]
                    im = links[1, mu, a, b, t]
                    re, im = cosine * re - sine * im, cosine * im + sine * re
                    re_one, im_one = pltpu.roll(re, nz - 1, 1), -pltpu.roll(im, nz - 1, 1)
                    for p in range(2):
                        L[p, 0, mu, a, b, t] = merge(t, re, re_one, p)
                        L[p, 1, mu, a, b, t] = merge(t, im, im_one, p)

        over_t(combine)

    def load_link(p, mu, t):
        return [[(L[p, 0, mu, a, b, t], L[p, 1, mu, a, b, t]) for b in range(3)] for a in range(3)]

    for group in (send[2:], fsend[1:]):
        for ref in group:
            ref[...] = jnp.zeros_like(ref)

    def start_field(t):
        for s in range(4):
            for a in range(3):
                for ri in range(2):
                    zero = src[ri, s, a, 0, t]
                    one = pltpu.roll(src[ri, s, a, 1, t], nz - 1, 1)
                    for p in range(2):
                        value = merge(t, zero, one, p)
                        S[p, ri, s, a, t] = value
                        V[0, p, ri, s, a, t] = value

    over_t(start_field)

    def copy_of(kind, m):
        k = kind // 2
        to = lower[k] if kind % 2 == 0 else upper[k]
        chain, slot = lax.rem(m, 2), lax.rem(m, 4)
        return pltpu.make_async_remote_copy(
            src_ref=send[kind].at[chain], dst_ref=recv[kind].at[slot],
            send_sem=send_sem.at[kind, chain], recv_sem=recv_sem.at[kind, slot],
            device_id=device(k, to), device_id_type=MESH)

    def force_copy(k, p):
        return pltpu.make_async_remote_copy(
            src_ref=fsend[k].at[p], dst_ref=frecv[k].at[p],
            send_sem=fsend_sem.at[k, p], recv_sem=frecv_sem.at[k, p],
            device_id=device(k, lower[k]), device_id_type=MESH)

    def slot_of(k, ri, t):
        i = ri * nt + t
        return (i // nx, i % nx) if k == 1 else (i // ny, i % ny)

    def pack(ref, half, k, t, ahead):
        for ri in range(2):
            tile, slot = slot_of(k, ri, t)
            if k == 1:
                shift = slot * ny if ahead else (slot + 1) * ny
                mask = row_x == slot
            else:
                shift = slot if ahead else slot + 1 + R - ny
                mask = row_y == slot
            shift = lax.rem(shift, R)
            for s in range(2):
                for a in range(3):
                    moved = pltpu.roll(half[s][a][ri], shift, 0)
                    ref[s, a, tile] = jnp.where(mask, moved, ref[s, a, tile])

    def shifted(half, ref, k, p, t, ahead):
        out = [[[None, None] for a in range(3)] for s in range(2)]
        if k == 1:
            own = R - ny if ahead else ny
            mask = row_x == (nx - 1 if ahead else 0)
            wraps = (last[1] if ahead else first[1]) == 1
            copy_zero = (corner + t + row_x + row_y + lane + p) % 2 == 0
        else:
            own = R - 1 if ahead else 1
            mask = row_y == (ny - 1 if ahead else 0)
        for ri in range(2):
            tile, slot = slot_of(k, ri, t)
            if k == 1:
                shift = (nx - 1 - slot) * ny if ahead else (nx - slot) * ny
            else:
                shift = ny - 1 - slot if ahead else R - slot
            shift = lax.rem(shift, R)
            for s in range(2):
                for a in range(3):
                    face = pltpu.roll(ref[s, a, tile], shift, 0)
                    if k == 1:
                        other = jnp.where(copy_zero, pltpu.roll(face, 1, 1),
                                          pltpu.roll(face, nz - 1, 1))
                        face = jnp.where(wraps, other, face)
                    out[s][a][ri] = jnp.where(mask, face, pltpu.roll(half[s][a][ri], own, 0))
        return out

    def z_ahead(half):
        return map_half(lambda h: pltpu.roll(h, nz - 1, 1), half)

    def z_behind(half):
        return map_half(lambda h: pltpu.roll(h, 1, 1), half)

    def ahead_face_t(field, ref, plus):
        half = project(load_spinor(field, 0), 0, plus)
        store_half(ref, map_half(lambda h: h * sign_ahead, half))

    def send_faces(field, p, m, behind):
        chain = lax.rem(m, 2)
        ahead_face_t(field, send[0].at[chain], False)
        copy_of(0, m).start()

        def behind_t():
            half = project(load_spinor(field, nt - 1), 0, True)
            half = color_apply(load_link(p, 0, nt - 1), half, True)
            store_half(send[1].at[chain], map_half(lambda h: h * sign_behind, half))
            copy_of(1, m).start()

        pl.when(behind)(behind_t)

        def face_xy(t):
            spinor = load_spinor(field, t)
            for k in (1, 2):
                pack(send[2 * k].at[chain], project(spinor, k, False), k, t, True)
                half = color_apply(load_link(p, k, t), project(spinor, k, True), True)
                store_half(PX.at[chain, k - 1], half, t)
                pack(send[2 * k + 1].at[chain], half, k, t, False)

        over_t(face_xy)
        copy_of(2, m).start()
        copy_of(4, m).start()

        def behind_xy():
            copy_of(3, m).start()
            copy_of(5, m).start()

        pl.when(behind)(behind_xy)

    rounds = 2 * DEGREE
    pl.semaphore_wait(barrier, 6)

    def first_faces(m, carry):
        send_faces(V.at[0, m], m, m, m >= 0)
        return carry

    lax.fori_loop(0, 2, first_faces, 0)

    def hop(m, carry):
        n = m // 2
        chain = lax.rem(m, 2)
        slot = lax.rem(m, 4)
        p = lax.rem(chain + n, 2)
        q = 1 - p
        now = V.at[lax.rem(n, 2), p]
        new = V.at[lax.rem(n + 1, 2), q]

        def along_z(t):
            total = load_spinor(S.at[q], t)
            spinor = load_spinor(now, t)
            half = color_apply(load_link(p, 3, t), project(spinor, 3, True), True)
            total = accumulate(total, z_behind(half), 3, True)
            half = z_ahead(project(spinor, 3, False))
            half = color_apply(load_link(q, 3, t), half, False)
            total = accumulate(total, half, 3, False)
            store_spinor(new, t, total)

        over_t(along_z)

        def along_t(t):
            half = project(load_spinor(now, t + 1), 0, False)
            half = color_apply(load_link(q, 0, t), half, False)
            store_spinor(new, t, accumulate(load_spinor(new, t), half, 0, False))
            half = color_apply(load_link(p, 0, t), project(load_spinor(now, t), 0, True), True)
            store_spinor(new, t + 1, accumulate(load_spinor(new, t + 1), half, 0, True))

        if nt > 1:
            over_t(along_t, nt - 1)

        for kind in range(2, 6):
            copy_of(kind, m).wait_recv()

        def along_xy(t):
            spinor = load_spinor(now, t)
            total = load_spinor(new, t)
            for k in (1, 2):
                half = shifted(project(spinor, k, False), recv[2 * k].at[slot], k, q, t, True)
                half = color_apply(load_link(q, k, t), half, False)
                total = accumulate(total, half, k, False)
                half = load_half(PX.at[chain, k - 1], t)
                half = shifted(half, recv[2 * k + 1].at[slot], k, q, t, False)
                total = accumulate(total, half, k, True)
            store_spinor(new, t, total)

        over_t(along_xy)

        for kind in range(2):
            copy_of(kind, m).wait_recv()
        half = color_apply(load_link(q, 0, nt - 1), load_half(recv[0].at[slot]), False)
        total = accumulate(load_spinor(new, nt - 1), half, 0, False)
        store_spinor(new, nt - 1, total)
        half = load_half(recv[1].at[slot])
        store_spinor(new, 0, accumulate(load_spinor(new, 0), half, 0, True))
        for kind in range(6):
            copy_of(kind, m).wait_send()

        @pl.when(n == DEGREE - 1)
        def _():
            def restart(t):
                values = load_spinor(new, t)
                values = values[:2] + map_half(lambda h: -h, values[2:])
                store_spinor(S.at[q], t, values)
                store_spinor(new, t, values)

            over_t(restart)

        send_faces(new, q, m + 2, n < rounds - 1)

        @pl.when(n == DEGREE - 1)
        def _():
            ahead_face_t(S.at[q], fsend[0].at[q], True)

            def face(t):
                spinor = load_spinor(S.at[q], t)
                for k in (1, 2):
                    pack(fsend[k].at[q], project(spinor, k, True), k, t, True)

            over_t(face)
        @pl.when(n == DEGREE + 1)
        def _():
            for k in (1, 2):
                force_copy(k, q).start()

        @pl.when(n == rounds - 1)
        def _():
            for k in (0,):
                force_copy(k, q).start()

        return carry

    lax.fori_loop(0, 2 * rounds, hop, 0)

    W = V.at[rounds % 2]

    def outer_into(out, left, right):
        for a in range(3):
            for b in range(3):
                for s in range(2):
                    lr, li = left[s][a]
                    rr, ri = right[s][b]
                    re = lr * rr + li * ri
                    im = li * rr - lr * ri
                    old = out[a][b]
                    out[a][b] = (re, im) if old is None else (old[0] + re, old[1] + im)
        return out

    def finish(mu, t, heads):
        parts = []
        for q in range(2):
            ahead_x, ahead_y = heads(1 - q)
            here_y = project(load_spinor(W.at[q], t), mu, True)
            here_x = project(load_spinor(S.at[q], t), mu, False)
            out = [[None] * 3 for _ in range(3)]
            out = outer_into(out, ahead_x, here_y)
            parts.append(outer_into(out, ahead_y, here_x))
        both, link = [], []
        for a in range(3):
            line, link_line = [], []
            for b in range(3):
                pair, link_pair = [], []
                for ri in range(2):
                    zero, one = parts[0][a][b][ri], parts[1][a][b][ri]
                    copy_one = pltpu.roll(merge(t, zero, one, 1), 1, 1)
                    copy_zero = merge(t, zero, one, 0)
                    pair.append(copy_zero + copy_one if ri == 0 else copy_zero - copy_one)
                    link_pair.append(merge(t, L[0, ri, mu, a, b, t], L[1, ri, mu, a, b, t], 0))
                line.append(pair)
                link_line.append(link_pair)
            both.append(line)
            link.append(link_line)
        merged = []
        for a in range(3):
            line = []
            for b in range(3):
                re = im = None
                for k in range(3):
                    lr, li = link[a][k]
                    br, bi = both[k][b]
                    tr, ti = lr * br - li * bi, lr * bi + li * br
                    re = tr if re is None else re + tr
                    im = ti if im is None else im + ti
                line.append((re, im))
            merged.append(line)
        trace = merged[0][0][1] + merged[1][1][1] + merged[2][2][1]
        third = trace * (1.0 / 3.0)
        photon[mu, t] = CHARGE * trace
        for a in range(3):
            force[0, mu, a, a, t] = jnp.zeros_like(trace)
            force[1, mu, a, a, t] = merged[a][a][1] - third
            for b in range(a + 1, 3):
                re = 0.5 * (merged[a][b][0] - merged[b][a][0])
                im = 0.5 * (merged[a][b][1] + merged[b][a][1])
                force[0, mu, a, b, t] = re
                force[0, mu, b, a, t] = -re
                force[1, mu, a, b, t] = im
                force[1, mu, b, a, t] = im

    def force_z(t):
        finish(3, t, lambda p: (z_ahead(project(load_spinor(S.at[p], t), 3, True)),
                                z_ahead(project(load_spinor(W.at[p], t), 3, False))))

    over_t(force_z)

    def force_t(t):
        finish(0, t, lambda p: (project(load_spinor(S.at[p], t + 1), 0, True),
                                project(load_spinor(W.at[p], t + 1), 0, False)))

    if nt > 1:
        over_t(force_t, nt - 1)

    numbers = [2 * rounds + (p + rounds) % 2 for p in range(2)]
    for k in (2, 1, 0):
        for p in range(2):
            force_copy(k, p).wait()
            copy_of(2 * k, numbers[p]).wait()
        if k == 0:
            finish(0, nt - 1, lambda p: (load_half(frecv[0].at[p]),
                                         load_half(recv[0].at[numbers[p] % 4])))
        else:
            def force_k(t):
                finish(k, t, lambda p: (
                    shifted(project(load_spinor(S.at[p], t), k, True), frecv[k].at[p],
                            k, 1 - p, t, True),
                    shifted(project(load_spinor(W.at[p], t), k, False),
                            recv[2 * k].at[numbers[p] % 4], k, 1 - p, t, True)))
            over_t(force_k)


def per_device(source, gauge_links, photon_angles):
    _, _, _, copies, nt, nx, ny, nz = source.shape
    R = nx * ny
    face = [(2, 2, 3, R, nz),
            (2, 3, -(-2 * nt // nx), R, nz),
            (2, 3, -(-2 * nt // ny), R, nz)]
    f32 = jnp.float32
    field = (2, 2, 4, 3, nt, R, nz)

    def vm(shape):
        return pltpu.VMEM(shape, f32)

    color, photon = pl.pallas_call(
        functools.partial(kernel, (copies, nt, nx, ny, nz)),
        out_shape=(jax.ShapeDtypeStruct((2, 4, 3, 3, nt, R, nz), f32),
                   jax.ShapeDtypeStruct((4, nt, R, nz), f32)),
        in_specs=[pl.BlockSpec(memory_space=pltpu.VMEM)] * 3,
        out_specs=(pl.BlockSpec(memory_space=pltpu.VMEM),) * 2,
        scratch_shapes=[
            vm((2, 2, 4, 3, 3, nt, R, nz)),
            vm(field),
            vm((2,) + field),
            vm((2, 2, 2, 2, 3, nt, R, nz)),
            [vm((2,) + face[kind // 2]) for kind in range(6)],
            [vm((4,) + face[kind // 2]) for kind in range(6)],
            [vm((2,) + face[k]) for k in range(3)],
            [vm((2,) + face[k]) for k in range(3)],
            pltpu.SemaphoreType.DMA((6, 2)),
            pltpu.SemaphoreType.DMA((6, 4)),
            pltpu.SemaphoreType.DMA((3, 2)),
            pltpu.SemaphoreType.DMA((3, 2)),
        ],
        compiler_params=pltpu.CompilerParams(
            collective_id=0, has_side_effects=True, vmem_limit_bytes=40 * 1024 * 1024),
    )(source.reshape(2, 4, 3, copies, nt, R, nz),
      gauge_links.reshape(2, 4, 3, 3, nt, R, nz),
      photon_angles.reshape(4, nt, R, nz))
    return (color.reshape(2, 4, 3, 3, nt, nx, ny, nz), photon.reshape(4, nt, nx, ny, nz))


def solution(mesh):
    in_specs = (
        P(None, None, None, None, "ta", "gx", "yz", None),
        P(None, None, None, None, "ta", "gx", "yz", None),
        P(None, "ta", "gx", "yz", None),
    )
    out_specs = (P(None, None, None, None, "ta", "gx", "yz", None), P(None, "ta", "gx", "yz", None))
    return jax.shard_map(
        per_device, mesh=mesh, in_specs=in_specs, out_specs=out_specs, check_vma=False
    )
```
